32 devices in a mesh: groups: 2 (over y), rows: 8 (over z, x), cols: 2 (over core).
Axes of the slice: x: 2, y: 2, z: 4, core: 2. Of those that a mesh axis runs over, the one named last changes fastest.
Arguments:
- inputs: bfloat16 [4, 32, 64, 512], P('groups', None, 'rows', 'cols'), parts along dimension 0, may hold values from -6 to 6
- hidden_init: bfloat16 [64, 64, 512], P('groups', 'rows', 'cols'), parts along dimension 0, may hold values from -3 to 3
- cell_init: bfloat16 [64, 64, 512], P('groups', 'rows', 'cols'), parts along dimension 0, may hold values from -6 to 6
- grad_hidden: bfloat16 [64, 64, 512], P('groups', 'rows', 'cols'), parts along dimension 0, may hold values from -6 to 6
- grad_cell: bfloat16 [64, 64, 512], P('groups', 'rows', 'cols'), parts along dimension 0, may hold values from -6 to 6
- depth_kernel: float32 [64, 25], replicated, may hold values from -1.25 to 1.25
- point_kernel: bfloat16 [64, 128], replicated, may hold values from -0.75 to 0.75
- gate_bias: float32 [128], replicated, may hold values from -4 to 4
Outputs:
- grad_hidden_init: bfloat16 [64, 64, 512], P('groups', 'rows', 'cols'), parts along dimension 0
- grad_cell_init: bfloat16 [64, 64, 512], P('groups', 'rows', 'cols'), parts along dimension 0
- grad_point: float32 [128, 128], P('groups'), parts along dimension 0
- grad_depth: float32 [128, 25], P('groups'), parts along dimension 0
- grad_bias: float32 [256], P('groups'), parts along dimension 0
The draws below stay inside these ranges and needn't reach their ends.
There are 2 independent parts, one for each index of `groups`. The reference program is written for one: setup_inputs(seed, part) draws one part's arguments, and reference() takes and returns one part's arrays. A program takes and returns all parts, laid end to end along the dimension named above; an argument that names none is the same for every part. Nothing has to cross between parts.
All inputs are finite; a program needn't handle non-finite values.
Results may differ from the reference program's by a relative error of at most 0.0062.
Values may be sent and summed in bfloat16 or wider, within the bound.
A program may use at most 64 MiB of HBM per device.

```python
import math
import jax
import jax.numpy as jnp
from jax import lax

IN = 32
HID = 32
KS = 5
STEPS = 2
H = 64
W = 512


def block_scale(stream_key, extent, split, least, top_value):
    gain, own = 1.0, jax.random.fold_in(stream_key, 6)
    for axis_at, blocks in split:
        draws = jnp.exp(jax.random.uniform(jax.random.fold_in(own, axis_at), (blocks,), jnp.float32, least / len(split), top_value / len(split)))
        gain = gain * jnp.repeat(draws, extent[axis_at] // blocks).reshape([-1 if axis == axis_at else 1 for axis in range(len(extent))])
    return gain


def scatter_about(rng, extent, scale, most, split=(), held_as=jnp.bfloat16):
    entries = jax.random.normal(rng, extent, jnp.float32) * scale
    if len(split) > 0:
        entries = block_scale(rng, extent, split, -0.22, 0.18) * entries
    return jnp.clip(entries, min=-most, max=most).astype(held_as)


def setup_inputs(seed: int = 0, part: int = 0) -> dict:
    seeds = jax.random.split(jax.random.key(seed), 9)
    own_keys = jax.random.split(jax.random.fold_in(seeds[8], part), 9)
    inputs = scatter_about(own_keys[0], (STEPS, IN, H, W), 1.0, 6.0, ((2, 8), (3, 2)))
    hidden_init = scatter_about(own_keys[1], (HID, H, W), 0.5, 3.0, ((1, 8), (2, 2)))
    cell_init = scatter_about(own_keys[2], (HID, H, W), 1.0, 6.0, ((1, 8), (2, 2)))
    grad_hidden = scatter_about(own_keys[3], (HID, H, W), 1.0, 6.0, ((1, 8), (2, 2)))
    grad_cell = scatter_about(own_keys[4], (HID, H, W), 1.0, 6.0, ((1, 8), (2, 2)))
    depth_kernel = scatter_about(seeds[5], (IN + HID, KS * KS), (KS * KS) ** -0.5, 1.25, (), jnp.float32)
    point_kernel = scatter_about(seeds[6], (IN + HID, 4 * HID), (IN + HID) ** -0.5, 0.75)
    gate_bias = scatter_about(seeds[7], (4 * HID,), 1.0, 4.0, (), jnp.float32)
    return {"inputs": inputs, "hidden_init": hidden_init, "cell_init": cell_init, "grad_hidden": grad_hidden, "grad_cell": grad_cell, "depth_kernel": depth_kernel, "point_kernel": point_kernel, "gate_bias": gate_bias}


def tap_sum(padded, kernel, row_count, col_count):
    wide = padded.astype(jnp.float32)
    summed = jnp.zeros((padded.shape[0], row_count, col_count), jnp.float32)
    for row_tap in range(5):
        for col_tap in range(5):
            weight_col = kernel[:, row_tap * 5 + col_tap][:, None, None]
            window = wide[:, row_tap:row_tap + row_count, col_tap:col_tap + col_count]
            summed = summed + weight_col * window
    return summed

def gate_math(gate_values, cell_prev):
    quarter = gate_values.shape[0] // 4
    ingate = jax.nn.sigmoid(gate_values[:quarter])
    forget = jax.nn.sigmoid(gate_values[quarter:2 * quarter])
    outgate = jax.nn.sigmoid(gate_values[2 * quarter:3 * quarter])
    update = jnp.tanh(gate_values[3 * quarter:])
    cell_state = forget * cell_prev + ingate * update
    return (outgate * jnp.tanh(cell_state), cell_state)

def gate_inputs(depth_flat, point_kernel, gate_bias):
    return lax.dot_general(point_kernel, depth_flat, (((0,), (0,)), ((), ())), preferred_element_type=jnp.float32) + gate_bias[:, None]

def backward_cell(depth_flat, cell_prev, grad_hid, grad_cel, point_kernel, gate_bias):
    gate_values = gate_inputs(depth_flat, point_kernel, gate_bias)
    unused_out, pullback = jax.vjp(gate_math, gate_values, cell_prev)
    grad_gates, grad_prev = pullback((grad_hid, grad_cel))
    gates_low = grad_gates.astype(jnp.bfloat16)
    grad_depth = jnp.dot(point_kernel, gates_low, preferred_element_type=jnp.float32).astype(jnp.bfloat16)
    grad_point = lax.dot_general(depth_flat, gates_low, (((1,), (1,)), ((), ())), preferred_element_type=jnp.float32)
    grad_bias = lax.optimization_barrier(jnp.sum(grad_gates, axis=1))
    return (grad_depth, grad_prev, grad_point, grad_bias)

def kernel_grad(grad_depth3, padded, row_count, col_count):
    grad_wide = grad_depth3.astype(jnp.float32)
    wide = padded.astype(jnp.float32)
    columns = []
    for row_tap in range(5):
        for col_tap in range(5):
            window = wide[:, row_tap:row_tap + row_count, col_tap:col_tap + col_count]
            columns.append(lax.optimization_barrier(jnp.sum(grad_wide * window, axis=(1, 2))))
    return jnp.stack(columns, axis=1)

def reference(inputs, hidden_init, cell_init, grad_hidden, grad_cell, depth_kernel, point_kernel, gate_bias):
    block_rows = math.gcd(H, 64)
    block_count = H // block_rows
    starts = jnp.arange(block_count, dtype=jnp.int32) * block_rows
    channels = hidden_init.shape[0]
    input_count = inputs.shape[1]
    flipped = depth_kernel[:, ::-1]

    def widen(field):
        return jnp.pad(field, ((0, 0), (2, 2), (2, 2)))

    def rejoin(stacked):
        return jnp.moveaxis(stacked, 0, 1).reshape(stacked.shape[1], H, W)

    def rows_of(field, first_row, row_count):
        return lax.dynamic_slice_in_dim(field, first_row, row_count, 1)

    def forward(padded, cell_prev):

        def one_block(first_row):
            window = rows_of(padded, first_row, block_rows + 4)
            depth_out = tap_sum(window, depth_kernel, block_rows, W).astype(jnp.bfloat16)
            depth_flat = depth_out.reshape(window.shape[0], -1)
            cell_block = rows_of(cell_prev, first_row, block_rows).reshape(channels, -1)
            hidden_new, cell_new = gate_math(gate_inputs(depth_flat, point_kernel, gate_bias), cell_block)
            return (hidden_new.astype(jnp.bfloat16).reshape(channels, block_rows, W), cell_new.reshape(channels, block_rows, W))
        hidden_blocks, cell_blocks = lax.map(one_block, starts)
        return (rejoin(hidden_blocks), rejoin(cell_blocks))

    def backward(padded, cell_prev, grad_hid, grad_cel):

        def one_block(first_row):
            window = rows_of(padded, first_row, block_rows + 4)
            depth_out = tap_sum(window, depth_kernel, block_rows, W).astype(jnp.bfloat16)
            depth_flat = depth_out.reshape(window.shape[0], -1)
            cell_block = rows_of(cell_prev, first_row, block_rows).reshape(channels, -1)
            hid_block = rows_of(grad_hid, first_row, block_rows).reshape(channels, -1)
            cel_block = rows_of(grad_cel, first_row, block_rows).reshape(channels, -1)
            grad_depth, grad_prev, grad_point, grad_bias = backward_cell(depth_flat, cell_block, hid_block, cel_block, point_kernel, gate_bias)
            grad_depth3 = grad_depth.reshape(window.shape[0], block_rows, W)
            grad_kernel = kernel_grad(grad_depth3, window, block_rows, W)
            return (grad_depth3, grad_prev.reshape(channels, block_rows, W), grad_point, grad_bias, grad_kernel)
        results = lax.map(one_block, starts)
        spread = widen(rejoin(results[0])[input_count:])

        def back_block(first_row):
            window = rows_of(spread, first_row, block_rows + 4)
            return tap_sum(window, flipped[input_count:], block_rows, W)
        grad_hidden_prev = rejoin(lax.map(back_block, starts))
        return (grad_hidden_prev, rejoin(results[1]), lax.optimization_barrier(jnp.sum(results[2], axis=0)), lax.optimization_barrier(jnp.sum(results[4], axis=0)), lax.optimization_barrier(jnp.sum(results[3], axis=0)))
    cell_start = cell_init.astype(jnp.float32)
    padded_first = widen(jnp.concatenate([inputs[0], hidden_init], axis=0))
    hidden_one, cell_one = forward(padded_first, cell_start)
    padded_second = widen(jnp.concatenate([inputs[1], hidden_one], axis=0))
    grad_hid_one, grad_cell_one, point_two, kernel_two, bias_two = backward(padded_second, cell_one, grad_hidden.astype(jnp.float32), grad_cell.astype(jnp.float32))
    grad_hid_zero, grad_cell_zero, point_one, kernel_one, bias_one = backward(padded_first, cell_start, grad_hid_one, grad_cell_one)
    grad_scale = 1.0 / math.sqrt(H * W)
    return (grad_hid_zero.astype(jnp.bfloat16), grad_cell_zero.astype(jnp.bfloat16), (point_one + point_two) * grad_scale, (kernel_one + kernel_two) * grad_scale, (bias_one + bias_two) * grad_scale)
```

```python
import functools
import math

import jax
import jax.numpy as jnp
from jax import lax
from jax.experimental import pallas as pl
from jax.experimental.pallas import tpu as pltpu
from jax.sharding import PartitionSpec as P

F32 = jnp.float32
BF16 = jnp.bfloat16
MESH = pl.DeviceIdType.MESH
LANES = 128
RIM = 2


def sigmoid(x):
    return 0.5 * jnp.tanh(0.5 * x) + 0.5


def kernel(
    dims,
    inputs, hidden_init, cell_init, grad_hidden, grad_cell, depth_kernel, point_kernel, gate_bias,
    out_hidden, out_cell, out_point, out_depth, out_bias,
    z_one, z_two, d_one, d_two,
    shift_one, shift_two, shift_back,
    taps, depth_wide, depth_low, grads_low, point_t, bias_wide,
    gates_one, cell_zero, cell_one, tanh_one, hid_grad, cel_grad, spread,
    depth_grad, tap_part, bias_part, point_part,
    pay, gathered, arrived,
    rim_send, rim_recv, sum_send, sum_recv, all_send, all_recv,
):
    n_rows, n_cols, rows, width, chans, scale = dims
    half = chans // 2
    n = n_rows * n_cols
    owners, chunk = arrived_shape(n)
    row = lax.axis_index("rows")
    col = lax.axis_index("cols")
    me = row * n_cols + col
    last = n_rows - 1
    edge = pl.ds(pl.multiple_of((1 - col) * (width - LANES), LANES), LANES)
    beyond = pl.ds(width, LANES)

    def place(index):
        return {"rows": index // n_cols, "cols": lax.rem(index, n_cols)}

    barrier = pltpu.get_barrier_semaphore()

    @pl.loop(1, n)
    def _(k):
        pl.semaphore_signal(
            barrier, inc=1, device_id=place(lax.rem(me + k, n)), device_id_type=MESH
        )

    def copies(buf, first, count, which):
        ch = pl.ds(first, count)
        own = pl.ds(0, width)
        up_src, up_dst = pl.ds(RIM, RIM), pl.ds(rows + RIM, RIM)
        down_src, down_dst = pl.ds(rows, RIM), pl.ds(0, RIM)
        mid = pl.ds(RIM, rows)

        def one(at, src_rows, dst_rows, src_cols, dst_cols, to_row, to_col):
            return pltpu.make_async_remote_copy(
                src_ref=buf.at[src_rows, ch, src_cols],
                dst_ref=buf.at[dst_rows, ch, dst_cols],
                send_sem=rim_send.at[which, at],
                recv_sem=rim_recv.at[which, at],
                device_id={"rows": to_row, "cols": to_col},
                device_id_type=MESH,
            )

        above, below = jnp.maximum(row - 1, 0), jnp.minimum(row + 1, last)
        side = one(0, mid, mid, edge, beyond, row, 1 - col)
        ups = [
            one(1, up_src, up_dst, own, own, above, col),
            one(2, up_src, up_dst, edge, beyond, above, 1 - col),
        ]
        downs = [
            one(3, down_src, down_dst, own, own, below, col),
            one(4, down_src, down_dst, edge, beyond, below, 1 - col),
        ]
        return side, ups, downs

    def start(group):
        side, ups, downs = group

        @pl.when(row > 0)
        def _():
            for item in ups:
                item.start()

        @pl.when(row < last)
        def _():
            for item in downs:
                item.start()

        side.start()

    def wait_recv(group):
        side, ups, downs = group
        side.wait_recv()

        @pl.when(row < last)
        def _():
            for item in ups:
                item.wait_recv()

        @pl.when(row > 0)
        def _():
            for item in downs:
                item.wait_recv()

    def wait_send(group):
        side, ups, downs = group
        side.wait_send()

        @pl.when(row > 0)
        def _():
            for item in ups:
                item.wait_send()

        @pl.when(row < last)
        def _():
            for item in downs:
                item.wait_send()

    def by_row(field):
        return jnp.swapaxes(field.astype(F32), 0, 1)

    mid = pl.ds(RIM, rows)
    own = pl.ds(0, width)
    low, high = pl.ds(0, half), pl.ds(half, half)
    z_one[mid, low, own] = by_row(inputs[0]).astype(BF16)
    z_one[mid, high, own] = by_row(hidden_init[...]).astype(BF16)
    z_two[mid, low, own] = by_row(inputs[1]).astype(BF16)
    for at, rim in ((0, pl.ds(0, RIM)), (last, pl.ds(rows + RIM, RIM))):

        @pl.when(row == at)
        def _():
            for buf in (z_one, z_two, d_one, d_two):
                buf[rim] = jnp.zeros((RIM,) + buf.shape[1:], BF16)

    pl.semaphore_wait(barrier, n - 1)
    first_rim = copies(z_one, 0, chans, 0)
    input_rim = copies(z_two, 0, half, 1)
    hidden_rim = copies(z_two, half, half, 2)
    two_rim = copies(d_two, 0, half, 3)
    one_rim = copies(d_one, 0, half, 4)
    start(first_rim)
    start(input_rim)

    cell_zero[...] = by_row(cell_init[...])
    hid_grad[...] = by_row(grad_hidden[...])
    cel_grad[...] = by_row(grad_cell[...])
    point_t[...] = jnp.transpose(point_kernel[...].astype(F32)).astype(BF16)
    bias_wide[...] = jnp.broadcast_to(jnp.transpose(gate_bias[...]), bias_wide.shape)
    for tap in range(25):
        taps[tap] = jnp.broadcast_to(depth_kernel[:, tap : tap + 1], taps.shape[1:])
    bias_part[...] = jnp.zeros_like(bias_part)

    lane = lax.broadcasted_iota(jnp.int32, (half, LANES), 1)
    least = col * (LANES - RIM)
    keep = jnp.logical_and(lane >= least, lane < least + RIM)

    def shift_rows(buf, first, into):
        ch = pl.ds(first, half)

        @pl.loop(0, rows + 2 * RIM)
        def _(at):
            mine = buf[at, ch, own].astype(F32)
            side = jnp.where(keep, buf[at, ch, beyond].astype(F32), 0.0)
            ring = jnp.concatenate([mine, side], axis=1)
            for tap in range(5):
                moved = pltpu.roll(ring, (RIM - tap) % ring.shape[1], 1) if tap != RIM else ring
                into[tap, at, ch, :] = moved[:, :width]

    def tap_sum(source, group, weight_at, flip):
        ch = pl.ds(pl.multiple_of(group * 8, 8), 8)
        wch = pl.ds(pl.multiple_of(weight_at + group * 8, 8), 8)
        total = None
        for col_tap in range(5):
            for row_tap in range(5):
                tap = row_tap * 5 + col_tap
                weight = taps[24 - tap if flip else tap, wch, :]
                term = weight[None] * source[col_tap, pl.ds(row_tap, rows), ch, :]
                total = term if total is None else total + term
        return total, ch

    def depth_of(source, groups):
        @pl.loop(*groups)
        def _(group):
            total, ch = tap_sum(source, group, 0, False)
            for at in range(rows):
                depth_wide[ch, pl.ds(at * width, width)] = total[at]

    def spread_of():
        @pl.loop(0, half // 8)
        def _(group):
            total, ch = tap_sum(shift_back, group, half, True)
            spread[:, ch, :] = total

    def gates_at(at, cells):
        low_depth = depth_wide[:, cells].astype(BF16)
        gates = jnp.dot(point_t[...], low_depth, preferred_element_type=F32) + bias_wide[...]
        i = sigmoid(gates[:half])
        f = sigmoid(gates[half : 2 * half])
        o = sigmoid(gates[2 * half : 3 * half])
        u = jnp.tanh(gates[3 * half :])
        return low_depth, i, f, o, u

    def cells_of(at):
        return pl.ds(pl.multiple_of(at * width, width), width)

    def back_at(at, d_buf, which, i, f, o, u, th, prev, dh, dc):
        dc = dc + dh * o * (1.0 - th * th)
        dg = jnp.concatenate(
            [
                dc * u * i * (1.0 - i),
                dc * prev * f * (1.0 - f),
                dh * th * o * (1.0 - o),
                dc * i * (1.0 - u * u),
            ],
            axis=0,
        )
        bias_part[...] += dg
        dg_low = dg.astype(BF16)
        grads_low[which, :, cells_of(at)] = dg_low
        dd = jnp.dot(point_kernel[...], dg_low, preferred_element_type=F32).astype(BF16)
        d_buf[at + RIM, :, own] = dd[half:]
        depth_grad[at] = dd.astype(F32)
        return dc * f

    def kernel_grad(source, begin):
        @pl.loop(0, chans // 8)
        def _(group):
            ch = pl.ds(pl.multiple_of(group * 8, 8), 8)
            grad = depth_grad[:, ch, :]
            for col_tap in range(5):
                for row_tap in range(5):
                    tap = row_tap * 5 + col_tap
                    both = jnp.sum(grad * source[col_tap, pl.ds(row_tap, rows), ch, :], axis=0)
                    part = both[:, :LANES]
                    for tile in range(1, width // LANES):
                        part = part + both[:, tile * LANES : (tile + 1) * LANES]
                    if begin:
                        tap_part[tap, ch, :] = part
                    else:
                        tap_part[tap, ch, :] += part

    def point_grad(which):
        return lax.dot_general(
            depth_low[which], grads_low[which], (((1,), (1,)), ((), ())), preferred_element_type=F32
        )

    wait_recv(first_rim)
    shift_rows(z_one, 0, shift_one)
    shift_rows(z_one, half, shift_one)
    depth_of(shift_one, (0, chans // 8))

    @pl.loop(0, rows, unroll=True)
    def _(at):
        cells = cells_of(at)
        low_depth, i, f, o, u = gates_at(at, cells)
        depth_low[0, :, cells] = low_depth
        c = f * cell_zero[at] + i * u
        th = jnp.tanh(c)
        z_two[at + RIM, high, own] = (o * th).astype(BF16)
        gates_one[at] = jnp.concatenate([i, f, o, u], axis=0)
        cell_one[at] = c
        tanh_one[at] = th

    start(hidden_rim)

    wait_recv(input_rim)
    shift_rows(z_two, 0, shift_two)
    depth_of(shift_two, (0, half // 8))
    wait_recv(hidden_rim)
    shift_rows(z_two, half, shift_two)
    depth_of(shift_two, (half // 8, chans // 8))

    @pl.loop(0, rows, unroll=True)
    def _(at):
        cells = cells_of(at)
        low_depth, i, f, o, u = gates_at(at, cells)
        depth_low[1, :, cells] = low_depth
        prev = cell_one[at]
        th = jnp.tanh(f * prev + i * u)
        cel_grad[at] = back_at(at, d_two, 1, i, f, o, u, th, prev, hid_grad[at], cel_grad[at])

    start(two_rim)
    kernel_grad(shift_two, True)
    point_part[...] = point_grad(1)
    wait_recv(two_rim)
    shift_rows(d_two, 0, shift_back)
    spread_of()

    @pl.loop(0, rows, unroll=True)
    def _(at):
        held = gates_one[at]
        i, f, o, u = (held[q * half : (q + 1) * half] for q in range(4))
        cel_grad[at] = back_at(
            at, d_one, 0, i, f, o, u, tanh_one[at], cell_zero[at], spread[at], cel_grad[at]
        )

    start(one_rim)
    kernel_grad(shift_one, False)
    point = (point_part[...] + point_grad(0)) * scale

    wide_lane = lax.broadcasted_iota(jnp.int32, (chans, LANES), 1)
    extra = jnp.zeros((chans, LANES), F32)
    for tap in range(25):
        sums = jnp.sum(tap_part[tap], axis=1, keepdims=True)
        extra = jnp.where(wide_lane == tap, sums, extra)
    bias_sum = jnp.sum(bias_part[...], axis=1, keepdims=True)
    extra = jnp.where(wide_lane == 25, bias_sum[:chans], extra)
    extra = jnp.where(wide_lane == 26, bias_sum[chans:], extra)
    pay[pl.ds(0, owners // 2)] = point.reshape(owners // 2, chunk, LANES)
    pay[pl.ds(owners // 2, owners // 2)] = (extra * scale).reshape(owners // 2, chunk, LANES)

    def scatter(k):
        owner = lax.rem(me + n - k, n)
        slot = jnp.minimum(owner, owners - 1)
        return owner, pltpu.make_async_remote_copy(
            src_ref=pay.at[slot],
            dst_ref=arrived.at[k - 1],
            send_sem=sum_send.at[k - 1],
            recv_sem=sum_recv.at[k - 1],
            device_id=place(owner),
            device_id_type=MESH,
        )

    def gather(k):
        return pltpu.make_async_remote_copy(
            src_ref=gathered.at[jnp.minimum(me, owners - 1)],
            dst_ref=gathered.at[jnp.minimum(me, owners - 1)],
            send_sem=all_send.at[k - 1],
            recv_sem=all_recv.at[k - 1],
            device_id=place(lax.rem(me + k, n)),
            device_id_type=MESH,
        )

    def owned(index, body):
        if owners == n:
            body()
        else:
            pl.when(index < owners)(body)

    @pl.loop(1, n)
    def _(k):
        owner, item = scatter(k)
        owned(owner, item.start)

    out_cell[...] = jnp.swapaxes(cel_grad[...], 0, 1).astype(BF16)
    wait_recv(one_rim)
    shift_rows(d_one, 0, shift_back)
    spread_of()
    out_hidden[...] = jnp.swapaxes(spread[...], 0, 1).astype(BF16)

    def reduce_own():
        @pl.loop(1, n)
        def _(k):
            scatter(k)[1].wait_recv()

        total = pay[jnp.minimum(me, owners - 1)] + jnp.sum(arrived[...], axis=0)
        gathered[jnp.minimum(me, owners - 1)] = total

        @pl.loop(1, n)
        def _(k):
            gather(k).start()

    owned(me, reduce_own)

    @pl.loop(1, n)
    def _(k):
        owned(lax.rem(me + n - k, n), lambda: gather(k).wait_recv())

    out_point[...] = gathered[pl.ds(0, owners // 2)].reshape(chans, LANES)
    rest = gathered[pl.ds(owners // 2, owners // 2)].reshape(chans, LANES)
    out_depth[...] = rest[:, :25]
    turned = jnp.transpose(rest)
    out_bias[...] = jnp.concatenate([turned[25:26], turned[26:27]], axis=1)

    for group in (first_rim, input_rim, hidden_rim, two_rim, one_rim):
        wait_send(group)

    @pl.loop(1, n)
    def _(k):
        owner, item = scatter(k)
        owned(owner, item.wait_send)

    def drain():
        @pl.loop(1, n)
        def _(k):
            gather(k).wait_send()

    owned(me, drain)


def arrived_shape(n):
    owners = min(n, 16)
    return owners, LANES // owners


def local(
    inputs, hidden_init, cell_init, grad_hidden, grad_cell, depth_kernel, point_kernel, gate_bias
):
    half, rows, width = hidden_init.shape
    chans = 2 * half
    n_rows, n_cols = lax.axis_size("rows"), lax.axis_size("cols")
    n = n_rows * n_cols
    owners, chunk = arrived_shape(n)
    scale = 1.0 / math.sqrt(rows * width * n)
    tall, wide = rows + 2 * RIM, width + LANES
    gates = 4 * half
    vm = pltpu.VMEM
    dma = pltpu.SemaphoreType.DMA
    outs = pl.pallas_call(
        functools.partial(kernel, (n_rows, n_cols, rows, width, chans, scale)),
        out_shape=[
            jax.ShapeDtypeStruct((half, rows, width), BF16),
            jax.ShapeDtypeStruct((half, rows, width), BF16),
            jax.ShapeDtypeStruct((chans, gates), F32),
            jax.ShapeDtypeStruct((chans, 25), F32),
            jax.ShapeDtypeStruct((1, gates), F32),
        ],
        in_specs=[pl.BlockSpec(memory_space=pltpu.VMEM)] * 8,
        out_specs=[pl.BlockSpec(memory_space=pltpu.VMEM)] * 5,
        scratch_shapes=[
            vm((tall, chans, wide), BF16),
            vm((tall, chans, wide), BF16),
            vm((tall, half, wide), BF16),
            vm((tall, half, wide), BF16),
            vm((5, tall, chans, width), F32),
            vm((5, tall, chans, width), F32),
            vm((5, tall, half, width), F32),
            vm((25, chans, width), F32),
            vm((chans, rows * width), F32),
            vm((2, chans, rows * width), BF16),
            vm((2, gates, rows * width), BF16),
            vm((gates, chans), BF16),
            vm((gates, width), F32),
            vm((rows, gates, width), F32),
            vm((rows, half, width), F32),
            vm((rows, half, width), F32),
            vm((rows, half, width), F32),
            vm((rows, half, width), F32),
            vm((rows, half, width), F32),
            vm((rows, half, width), F32),
            vm((rows, chans, width), F32),
            vm((25, chans, LANES), F32),
            vm((gates, width), F32),
            vm((chans, gates), F32),
            vm((owners, chunk, LANES), F32),
            vm((owners, chunk, LANES), F32),
            vm((n - 1, chunk, LANES), F32),
            dma((5, 5)),
            dma((5, 5)),
            dma((n - 1,)),
            dma((n - 1,)),
            dma((n - 1,)),
            dma((n - 1,)),
        ],
        compiler_params=pltpu.CompilerParams(
            collective_id=0, has_side_effects=True, vmem_limit_bytes=50 * 1024 * 1024
        ),
        name="surrogate",
    )(
        inputs, hidden_init, cell_init, grad_hidden, grad_cell, depth_kernel, point_kernel,
        gate_bias.reshape(1, -1),
    )
    return (*outs[:4], outs[4].reshape(-1))


def solution(mesh):
    placed = (
        P("groups", None, "rows", "cols"),
        P("groups", "rows", "cols"),
        P("groups", "rows", "cols"),
        P("groups", "rows", "cols"),
        P("groups", "rows", "cols"),
        P(),
        P(),
        P(),
    )
    return jax.shard_map(
        local,
        mesh=mesh,
        in_specs=placed,
        out_specs=(
            P("groups", "rows", "cols"),
            P("groups", "rows", "cols"),
            P("groups", None),
            P("groups", None),
            P("groups"),
        ),
        check_vma=False,
    )
```

```python
import functools
import math

import jax
import jax.numpy as jnp
from jax import lax
from jax.experimental import pallas as pl
from jax.experimental.pallas import tpu as pltpu
from jax.sharding import PartitionSpec as P

F32 = jnp.float32
BF16 = jnp.bfloat16
MESH = pl.DeviceIdType.MESH
LANES = 128
RIM = 2


def sigmoid(x):
    return 0.5 * jnp.tanh(0.5 * x) + 0.5


def kernel(
    dims,
    inputs_hbm, hidden_hbm, cell_hbm, grad_hidden_hbm, grad_cell_hbm, depth_hbm, point_hbm, bias_hbm,
    out_hidden, out_cell, out_point, out_depth, out_bias,
    inputs, hidden_init, cell_init, grad_hidden, grad_cell, depth_kernel, point_kernel, gate_bias,
    z_one, z_two, d_one, d_two,
    shift_one, shift_two, shift_back,
    taps, depth_wide, depth_low, grads_low, point_t, bias_wide,
    gates_one, cell_zero, cell_one, tanh_one, hid_grad, cel_grad, spread,
    depth_grad, tap_part, bias_part, point_part,
    pay, gathered, arrived,
    rim_send, rim_recv, sum_send, sum_recv, all_send, all_recv, load_sem, known,
):
    n_rows, n_cols, rows, width, chans, scale = dims
    half = chans // 2
    n = n_rows * n_cols
    owners, chunk = arrived_shape(n)
    row = lax.axis_index("rows")
    col = lax.axis_index("cols")
    me = row * n_cols + col
    last = n_rows - 1
    edge = pl.ds(pl.multiple_of((1 - col) * (width - LANES), LANES), LANES)
    beyond = pl.ds(width, LANES)

    def place(index):
        return {"rows": index // n_cols, "cols": lax.rem(index, n_cols)}

    barrier = pltpu.get_barrier_semaphore()

    has_up, has_down = row > 0, row < last

    def tell(sem, to_row, to_col):
        pl.semaphore_signal(
            sem, inc=1, device_id={"rows": to_row, "cols": to_col}, device_id_type=MESH
        )

    tell(barrier, row, 1 - col)

    @pl.when(has_up)
    def _():
        tell(barrier, row - 1, col)
        tell(barrier, row - 1, 1 - col)

    @pl.when(has_down)
    def _():
        tell(barrier, row + 1, col)
        tell(barrier, row + 1, 1 - col)

    loads = [
        pltpu.make_async_copy(src, dst, load_sem.at[at])
        for at, (src, dst) in enumerate(
            [
                (inputs_hbm.at[0], inputs.at[0]),
                (hidden_hbm, hidden_init),
                (inputs_hbm.at[1], inputs.at[1]),
                (cell_hbm, cell_init),
                (grad_hidden_hbm, grad_hidden),
                (grad_cell_hbm, grad_cell),
                (depth_hbm, depth_kernel),
                (point_hbm, point_kernel),
                (bias_hbm, gate_bias),
            ]
        )
    ]
    for item in loads:
        item.start()

    distances = [d for d in (2**p for p in range(1, 16)) if d < n_rows]

    def tell_far(level):
        d = distances[level]
        for ahead, to_row in ((row >= d, row - d), (row + d <= last, row + d)):

            @pl.when(ahead)
            def _():
                tell(known.at[level], jnp.clip(to_row, 0, last), col)

    def hear_far(level):
        d = distances[level]
        count = (row >= d).astype(jnp.int32) + (row + d <= last).astype(jnp.int32)
        pl.semaphore_wait(known.at[level], count)

    def copies(buf, first, count, which):
        ch = pl.ds(first, count)
        own = pl.ds(0, width)
        up_src, up_dst = pl.ds(RIM, RIM), pl.ds(rows + RIM, RIM)
        down_src, down_dst = pl.ds(rows, RIM), pl.ds(0, RIM)
        mid = pl.ds(RIM, rows)

        def one(at, src_rows, dst_rows, src_cols, dst_cols, to_row, to_col):
            return pltpu.make_async_remote_copy(
                src_ref=buf.at[src_rows, ch, src_cols],
                dst_ref=buf.at[dst_rows, ch, dst_cols],
                send_sem=rim_send.at[which, at],
                recv_sem=rim_recv.at[which, at],
                device_id={"rows": to_row, "cols": to_col},
                device_id_type=MESH,
            )

        above, below = jnp.maximum(row - 1, 0), jnp.minimum(row + 1, last)
        side = one(0, mid, mid, edge, beyond, row, 1 - col)
        ups = [
            one(1, up_src, up_dst, own, own, above, col),
            one(2, up_src, up_dst, edge, beyond, above, 1 - col),
        ]
        downs = [
            one(3, down_src, down_dst, own, own, below, col),
            one(4, down_src, down_dst, edge, beyond, below, 1 - col),
        ]
        return side, ups, downs

    def start(group):
        side, ups, downs = group
        side.start()

        @pl.when(row > 0)
        def _():
            for item in ups:
                item.start()

        @pl.when(row < last)
        def _():
            for item in downs:
                item.start()

    def wait_side(group):
        group[0].wait_recv()

    def wait_rows(group):
        _, ups, downs = group

        @pl.when(row < last)
        def _():
            for item in ups:
                item.wait_recv()

        @pl.when(row > 0)
        def _():
            for item in downs:
                item.wait_recv()

    def wait_send(group):
        side, ups, downs = group
        side.wait_send()

        @pl.when(row > 0)
        def _():
            for item in ups:
                item.wait_send()

        @pl.when(row < last)
        def _():
            for item in downs:
                item.wait_send()

    def by_row(field):
        return jnp.swapaxes(field.astype(F32), 0, 1)

    mid = pl.ds(RIM, rows)
    own = pl.ds(0, width)
    low, high = pl.ds(0, half), pl.ds(half, half)
    loads[0].wait()
    z_one[mid, low, own] = by_row(inputs[0]).astype(BF16)
    loads[1].wait()
    z_one[mid, high, own] = by_row(hidden_init[...]).astype(BF16)
    for at, rim in ((0, pl.ds(0, RIM)), (last, pl.ds(rows + RIM, RIM))):

        @pl.when(row == at)
        def _():
            for buf in (z_one, z_two, d_one, d_two):
                buf[rim] = jnp.zeros((RIM,) + buf.shape[1:], BF16)

    pl.semaphore_wait(barrier, 1 + 2 * has_up.astype(jnp.int32) + 2 * has_down.astype(jnp.int32))
    first_rim = copies(z_one, 0, chans, 0)
    input_rim = copies(z_two, 0, half, 1)
    hidden_rim = copies(z_two, half, half, 2)
    two_rim = copies(d_two, 0, half, 3)
    one_rim = copies(d_one, 0, half, 4)
    start(first_rim)

    for item in loads[2:]:
        item.wait()
    z_two[mid, low, own] = by_row(inputs[1]).astype(BF16)
    cell_zero[...] = by_row(cell_init[...])
    hid_grad[...] = by_row(grad_hidden[...])
    cel_grad[...] = by_row(grad_cell[...])
    point_t[...] = jnp.transpose(point_kernel[...].astype(F32)).astype(BF16)
    bias_wide[...] = jnp.broadcast_to(jnp.transpose(gate_bias[...]), bias_wide.shape)
    tap_cols = jnp.transpose(depth_kernel[...])
    for tap in range(25):
        taps[tap] = jnp.broadcast_to(tap_cols[:, tap : tap + 1], taps.shape[1:])
    bias_part[...] = jnp.zeros_like(bias_part)

    lane = lax.broadcasted_iota(jnp.int32, (half, LANES), 1)
    least = col * (LANES - RIM)
    keep = jnp.logical_and(lane >= least, lane < least + RIM)

    def shift_mid(buf, first, into):
        shift_rows(buf, first, into, RIM, rows)

    def shift_ends(buf, first, into):
        shift_rows(buf, first, into, 0, RIM)
        shift_rows(buf, first, into, rows + RIM, RIM)

    def shift_rows(buf, first, into, begin, count):
        ch = pl.ds(first, half)

        @pl.loop(begin, begin + count, unroll=2)
        def _(at):
            mine = buf[at, ch, own].astype(F32)
            side = jnp.where(keep, buf[at, ch, beyond].astype(F32), 0.0)
            ring = jnp.concatenate([mine, side], axis=1)
            for tap in range(5):
                moved = pltpu.roll(ring, (RIM - tap) % ring.shape[1], 1) if tap != RIM else ring
                into[tap, at, ch, :] = moved[:, :width]

    inner = [(RIM, rows - 2 * RIM)]
    outer = [(0, RIM), (rows - RIM, RIM)]

    def tap_sum(source, group, weight_at, flip, begin, count):
        ch = pl.ds(pl.multiple_of(group * 8, 8), 8)
        wch = pl.ds(pl.multiple_of(weight_at + group * 8, 8), 8)
        total = None
        for col_tap in range(5):
            for row_tap in range(5):
                tap = row_tap * 5 + col_tap
                weight = taps[24 - tap if flip else tap, wch, :]
                term = weight[None] * source[col_tap, pl.ds(begin + row_tap, count), ch, :]
                total = term if total is None else total + term
        return total, ch

    def depth_of(source, groups, parts):
        @pl.loop(*groups)
        def _(group):
            for begin, count in parts:
                total, ch = tap_sum(source, group, 0, False, begin, count)
                for at in range(count):
                    depth_wide[ch, pl.ds((begin + at) * width, width)] = total[at]

    def spread_of(parts):
        @pl.loop(0, half // 8)
        def _(group):
            for begin, count in parts:
                total, ch = tap_sum(shift_back, group, half, True, begin, count)
                spread[pl.ds(begin, count), ch, :] = total

    def gates_at(at, cells):
        low_depth = depth_wide[:, cells].astype(BF16)
        gates = jnp.dot(point_t[...], low_depth, preferred_element_type=F32) + bias_wide[...]
        i = sigmoid(gates[:half])
        f = sigmoid(gates[half : 2 * half])
        o = sigmoid(gates[2 * half : 3 * half])
        u = jnp.tanh(gates[3 * half :])
        return low_depth, i, f, o, u

    def cells_of(at):
        return pl.ds(pl.multiple_of(at * width, width), width)

    def back_at(at, d_buf, which, i, f, o, u, th, prev, dh, dc):
        dc = dc + dh * o * (1.0 - th * th)
        dg = jnp.concatenate(
            [
                dc * u * i * (1.0 - i),
                dc * prev * f * (1.0 - f),
                dh * th * o * (1.0 - o),
                dc * i * (1.0 - u * u),
            ],
            axis=0,
        )
        bias_part[...] += dg
        dg_low = dg.astype(BF16)
        grads_low[which, :, cells_of(at)] = dg_low
        dd = jnp.dot(point_kernel[...], dg_low, preferred_element_type=F32).astype(BF16)
        d_buf[at + RIM, :, own] = dd[half:]
        depth_grad[at] = dd.astype(F32)
        return dc * f

    def kernel_grad(source, begin):
        @pl.loop(0, chans // 8)
        def _(group):
            ch = pl.ds(pl.multiple_of(group * 8, 8), 8)
            grad = depth_grad[:, ch, :]
            for col_tap in range(5):
                for row_tap in range(5):
                    tap = row_tap * 5 + col_tap
                    both = jnp.sum(grad * source[col_tap, pl.ds(row_tap, rows), ch, :], axis=0)
                    part = both[:, :LANES]
                    for tile in range(1, width // LANES):
                        part = part + both[:, tile * LANES : (tile + 1) * LANES]
                    if begin:
                        tap_part[tap, ch, :] = part
                    else:
                        tap_part[tap, ch, :] += part

    def point_grad(which):
        return lax.dot_general(
            depth_low[which], grads_low[which], (((1,), (1,)), ((), ())), preferred_element_type=F32
        )

    every, first, second = (0, chans // 8), (0, half // 8), (half // 8, chans // 8)
    wait_side(first_rim)
    shift_mid(z_one, 0, shift_one)
    shift_mid(z_one, half, shift_one)
    depth_of(shift_one, every, inner)
    wait_rows(first_rim)
    start(input_rim)
    tell_far(0)
    shift_ends(z_one, 0, shift_one)
    shift_ends(z_one, half, shift_one)
    depth_of(shift_one, every, outer)

    @pl.loop(0, rows, unroll=True)
    def _(at):
        cells = cells_of(at)
        low_depth, i, f, o, u = gates_at(at, cells)
        depth_low[0, :, cells] = low_depth
        c = f * cell_zero[at] + i * u
        th = jnp.tanh(c)
        z_two[at + RIM, high, own] = (o * th).astype(BF16)
        gates_one[at] = jnp.concatenate([i, f, o, u], axis=0)
        cell_one[at] = c
        tanh_one[at] = th

    start(hidden_rim)

    wait_side(input_rim)
    wait_rows(input_rim)
    shift_mid(z_two, 0, shift_two)
    shift_ends(z_two, 0, shift_two)
    depth_of(shift_two, first, inner + outer)
    wait_side(hidden_rim)
    shift_mid(z_two, half, shift_two)
    depth_of(shift_two, second, inner)
    wait_rows(hidden_rim)
    hear_far(0)
    for level in range(1, len(distances)):
        if level > 1:
            hear_far(level - 1)
        tell_far(level)
    shift_ends(z_two, half, shift_two)
    depth_of(shift_two, second, outer)

    @pl.loop(0, rows, unroll=True)
    def _(at):
        cells = cells_of(at)
        low_depth, i, f, o, u = gates_at(at, cells)
        depth_low[1, :, cells] = low_depth
        prev = cell_one[at]
        th = jnp.tanh(f * prev + i * u)
        cel_grad[at] = back_at(at, d_two, 1, i, f, o, u, th, prev, hid_grad[at], cel_grad[at])

    start(two_rim)
    kernel_grad(shift_two, True)
    wait_side(two_rim)
    shift_mid(d_two, 0, shift_back)
    spread_of(inner)
    point_part[...] = point_grad(1)
    wait_rows(two_rim)
    if len(distances) > 1:
        hear_far(len(distances) - 1)
    shift_ends(d_two, 0, shift_back)
    spread_of(outer)

    @pl.loop(0, rows, unroll=True)
    def _(at):
        held = gates_one[at]
        i, f, o, u = (held[q * half : (q + 1) * half] for q in range(4))
        cel_grad[at] = back_at(
            at, d_one, 0, i, f, o, u, tanh_one[at], cell_zero[at], spread[at], cel_grad[at]
        )

    start(one_rim)
    kernel_grad(shift_one, False)
    point = (point_part[...] + point_grad(0)) * scale

    wide_lane = lax.broadcasted_iota(jnp.int32, (chans, LANES), 1)
    extra = jnp.zeros((chans, LANES), F32)
    for tap in range(25):
        sums = jnp.sum(tap_part[tap], axis=1, keepdims=True)
        extra = jnp.where(wide_lane == tap, sums, extra)
    bias_sum = jnp.sum(bias_part[...], axis=1, keepdims=True)
    extra = jnp.where(wide_lane == 25, bias_sum[:chans], extra)
    extra = jnp.where(wide_lane == 26, bias_sum[chans:], extra)
    pay[pl.ds(0, owners // 2)] = point.reshape(owners // 2, chunk, LANES)
    pay[pl.ds(owners // 2, owners // 2)] = (extra * scale).reshape(owners // 2, chunk, LANES)

    def scatter(k):
        owner = lax.rem(me + n - k, n)
        slot = jnp.minimum(owner, owners - 1)
        return owner, pltpu.make_async_remote_copy(
            src_ref=pay.at[slot],
            dst_ref=arrived.at[k - 1],
            send_sem=sum_send.at[k - 1],
            recv_sem=sum_recv.at[k - 1],
            device_id=place(owner),
            device_id_type=MESH,
        )

    def gather(k):
        return pltpu.make_async_remote_copy(
            src_ref=gathered.at[jnp.minimum(me, owners - 1)],
            dst_ref=gathered.at[jnp.minimum(me, owners - 1)],
            send_sem=all_send.at[k - 1],
            recv_sem=all_recv.at[k - 1],
            device_id=place(lax.rem(me + k, n)),
            device_id_type=MESH,
        )

    def owned(index, body):
        if owners == n:
            body()
        else:
            pl.when(index < owners)(body)

    @pl.loop(1, n)
    def _(k):
        owner, item = scatter(k)
        owned(owner, item.start)

    out_cell[...] = jnp.swapaxes(cel_grad[...], 0, 1).astype(BF16)
    wait_side(one_rim)
    shift_mid(d_one, 0, shift_back)
    spread_of(inner)
    wait_rows(one_rim)
    shift_ends(d_one, 0, shift_back)
    spread_of(outer)
    out_hidden[...] = jnp.swapaxes(spread[...], 0, 1).astype(BF16)

    def reduce_own():
        @pl.loop(1, n)
        def _(k):
            scatter(k)[1].wait_recv()

        total = pay[jnp.minimum(me, owners - 1)] + jnp.sum(arrived[...], axis=0)
        gathered[jnp.minimum(me, owners - 1)] = total

        @pl.loop(1, n)
        def _(k):
            gather(k).start()

    owned(me, reduce_own)

    @pl.loop(1, n)
    def _(k):
        owned(lax.rem(me + n - k, n), lambda: gather(k).wait_recv())

    out_point[...] = gathered[pl.ds(0, owners // 2)].reshape(chans, LANES)
    rest = gathered[pl.ds(owners // 2, owners // 2)].reshape(chans, LANES)
    turned = jnp.transpose(rest)
    out_depth[...] = turned[:25]
    out_bias[...] = jnp.concatenate([turned[25:26], turned[26:27]], axis=1)

    for group in (first_rim, input_rim, hidden_rim, two_rim, one_rim):
        wait_send(group)

    @pl.loop(1, n)
    def _(k):
        owner, item = scatter(k)
        owned(owner, item.wait_send)

    def drain():
        @pl.loop(1, n)
        def _(k):
            gather(k).wait_send()

    owned(me, drain)


def hand_over(*refs):
    sems = refs[10]
    items = [pltpu.make_async_copy(refs[at], refs[5 + at], sems.at[at]) for at in range(5)]
    for item in items:
        item.start()
    for item in items:
        item.wait()


def arrived_shape(n):
    owners = min(n, 16)
    return owners, LANES // owners


def local(
    inputs, hidden_init, cell_init, grad_hidden, grad_cell, depth_kernel, point_kernel, gate_bias
):
    half, rows, width = hidden_init.shape
    chans = 2 * half
    n_rows, n_cols = lax.axis_size("rows"), lax.axis_size("cols")
    n = n_rows * n_cols
    owners, chunk = arrived_shape(n)
    scale = 1.0 / math.sqrt(rows * width * n)
    tall, wide = rows + 2 * RIM, width + LANES
    gates = 4 * half
    vm = pltpu.VMEM
    dma = pltpu.SemaphoreType.DMA
    outs = pl.pallas_call(
        functools.partial(kernel, (n_rows, n_cols, rows, width, chans, scale)),
        out_shape=[
            jax.ShapeDtypeStruct((half, rows, width), BF16),
            jax.ShapeDtypeStruct((half, rows, width), BF16),
            jax.ShapeDtypeStruct((chans, gates), F32),
            jax.ShapeDtypeStruct((25, chans), F32),
            jax.ShapeDtypeStruct((1, gates), F32),
        ],
        in_specs=[pl.BlockSpec(memory_space=pl.ANY)] * 8,
        out_specs=[pl.BlockSpec(memory_space=pltpu.VMEM)] * 5,
        scratch_shapes=[
            vm(inputs.shape, BF16),
            vm((half, rows, width), BF16),
            vm((half, rows, width), BF16),
            vm((half, rows, width), BF16),
            vm((half, rows, width), BF16),
            vm((25, chans), F32),
            vm((chans, gates), BF16),
            vm((1, gates), F32),
            vm((tall, chans, wide), BF16),
            vm((tall, chans, wide), BF16),
            vm((tall, half, wide), BF16),
            vm((tall, half, wide), BF16),
            vm((5, tall, chans, width), F32),
            vm((5, tall, chans, width), F32),
            vm((5, tall, half, width), F32),
            vm((25, chans, width), F32),
            vm((chans, rows * width), F32),
            vm((2, chans, rows * width), BF16),
            vm((2, gates, rows * width), BF16),
            vm((gates, chans), BF16),
            vm((gates, width), F32),
            vm((rows, gates, width), F32),
            vm((rows, half, width), F32),
            vm((rows, half, width), F32),
            vm((rows, half, width), F32),
            vm((rows, half, width), F32),
            vm((rows, half, width), F32),
            vm((rows, half, width), F32),
            vm((rows, chans, width), F32),
            vm((25, chans, LANES), F32),
            vm((gates, width), F32),
            vm((chans, gates), F32),
            vm((owners, chunk, LANES), F32),
            vm((owners, chunk, LANES), F32),
            vm((n - 1, chunk, LANES), F32),
            dma((5, 5)),
            dma((5, 5)),
            dma((n - 1,)),
            dma((n - 1,)),
            dma((n - 1,)),
            dma((n - 1,)),
            dma((9,)),
            pltpu.SemaphoreType.REGULAR((max(1, (n_rows - 1).bit_length() - 1),)),
        ],
        compiler_params=pltpu.CompilerParams(
            collective_id=0, has_side_effects=True, vmem_limit_bytes=50 * 1024 * 1024
        ),
        name="surrogate",
    )(
        inputs, hidden_init, cell_init, grad_hidden, grad_cell, depth_kernel.T, point_kernel,
        gate_bias.reshape(1, -1),
    )
    outs = pl.pallas_call(
        hand_over,
        out_shape=[jax.ShapeDtypeStruct(out.shape, out.dtype) for out in outs],
        in_specs=[pl.BlockSpec(memory_space=pl.ANY)] * 5,
        out_specs=[pl.BlockSpec(memory_space=pl.ANY)] * 5,
        scratch_shapes=[dma((5,))],
        name="hand_over",
    )(*outs)
    return (*outs[:3], outs[3].T, outs[4].reshape(-1))


def solution(mesh):
    placed = (
        P("groups", None, "rows", "cols"),
        P("groups", "rows", "cols"),
        P("groups", "rows", "cols"),
        P("groups", "rows", "cols"),
        P("groups", "rows", "cols"),
        P(),
        P(),
        P(),
    )
    return jax.shard_map(
        local,
        mesh=mesh,
        in_specs=placed,
        out_specs=(
            P("groups", "rows", "cols"),
            P("groups", "rows", "cols"),
            P("groups", None),
            P("groups", None),
            P("groups"),
        ),
        check_vma=False,
    )
```

```python
import functools
import math

import jax
import jax.numpy as jnp
from jax import lax
from jax.experimental import pallas as pl
from jax.experimental.pallas import tpu as pltpu
from jax.sharding import PartitionSpec as P

F32 = jnp.float32
BF16 = jnp.bfloat16
MESH = pl.DeviceIdType.MESH
LANES = 128
RIM = 2


def sigmoid(x):
    return 0.5 * jnp.tanh(0.5 * x) + 0.5


def kernel(
    dims,
    inputs_hbm, hidden_hbm, cell_hbm, grad_hidden_hbm, grad_cell_hbm, depth_hbm, point_hbm, bias_hbm,
    out_hidden, out_cell, out_point, out_depth, out_bias,
    inputs, hidden_init, cell_init, grad_hidden, grad_cell, depth_kernel, point_kernel, gate_bias,
    z_one, z_two, d_one, d_two,
    shift_one, shift_two, shift_back,
    taps, depth_wide, depth_low, grads_low, point_t, bias_wide,
    gates_one, cell_zero, cell_one, tanh_one, hid_grad, cel_grad, spread,
    depth_grad, tap_part, bias_part, point_part,
    pay, gathered, arrived,
    rim_send, rim_recv, sum_send, sum_recv, all_send, all_recv, load_sem, known,
):
    n_rows, n_cols, rows, width, chans, scale = dims
    half = chans // 2
    n = n_rows * n_cols
    owners, chunk = arrived_shape(n)
    row = lax.axis_index("rows")
    col = lax.axis_index("cols")
    me = row * n_cols + col
    last = n_rows - 1
    edge = pl.ds(pl.multiple_of((1 - col) * (width - LANES), LANES), LANES)
    beyond = pl.ds(width, LANES)

    def place(index):
        return {"rows": index // n_cols, "cols": lax.rem(index, n_cols)}

    barrier = pltpu.get_barrier_semaphore()

    has_up, has_down = row > 0, row < last

    def tell(sem, to_row, to_col):
        pl.semaphore_signal(
            sem, inc=1, device_id={"rows": to_row, "cols": to_col}, device_id_type=MESH
        )

    tell(barrier, row, 1 - col)

    @pl.when(has_up)
    def _():
        tell(barrier, row - 1, col)
        tell(barrier, row - 1, 1 - col)

    @pl.when(has_down)
    def _():
        tell(barrier, row + 1, col)
        tell(barrier, row + 1, 1 - col)

    loads = [
        pltpu.make_async_copy(src, dst, load_sem.at[at])
        for at, (src, dst) in enumerate(
            [
                (inputs_hbm.at[0], inputs.at[0]),
                (hidden_hbm, hidden_init),
                (inputs_hbm.at[1], inputs.at[1]),
                (cell_hbm, cell_init),
                (grad_hidden_hbm, grad_hidden),
                (grad_cell_hbm, grad_cell),
                (depth_hbm, depth_kernel),
                (point_hbm, point_kernel),
                (bias_hbm, gate_bias),
            ]
        )
    ]
    for item in loads:
        item.start()

    distances = [d for d in (2**p for p in range(1, 16)) if d < n_rows]

    def tell_far(level):
        d = distances[level]
        for ahead, to_row in ((row >= d, row - d), (row + d <= last, row + d)):

            @pl.when(ahead)
            def _():
                tell(known.at[level], jnp.clip(to_row, 0, last), col)

    def hear_far(level):
        d = distances[level]
        count = (row >= d).astype(jnp.int32) + (row + d <= last).astype(jnp.int32)
        pl.semaphore_wait(known.at[level], count)

    def copies(buf, first, count, which):
        ch = pl.ds(first, count)
        own = pl.ds(0, width)
        up_src, up_dst = pl.ds(RIM, RIM), pl.ds(rows + RIM, RIM)
        down_src, down_dst = pl.ds(rows, RIM), pl.ds(0, RIM)
        mid = pl.ds(RIM, rows)

        def one(at, src_rows, dst_rows, src_cols, dst_cols, to_row, to_col):
            return pltpu.make_async_remote_copy(
                src_ref=buf.at[src_rows, ch, src_cols],
                dst_ref=buf.at[dst_rows, ch, dst_cols],
                send_sem=rim_send.at[which, at],
                recv_sem=rim_recv.at[which, at],
                device_id={"rows": to_row, "cols": to_col},
                device_id_type=MESH,
            )

        above, below = jnp.maximum(row - 1, 0), jnp.minimum(row + 1, last)
        side = one(0, mid, mid, edge, beyond, row, 1 - col)
        ups = [
            one(1, up_src, up_dst, own, own, above, col),
            one(2, up_src, up_dst, edge, beyond, above, 1 - col),
        ]
        downs = [
            one(3, down_src, down_dst, own, own, below, col),
            one(4, down_src, down_dst, edge, beyond, below, 1 - col),
        ]
        return side, ups, downs

    def start(group):
        side, ups, downs = group
        side.start()

        @pl.when(row > 0)
        def _():
            for item in ups:
                item.start()

        @pl.when(row < last)
        def _():
            for item in downs:
                item.start()

    def wait_side(group):
        group[0].wait_recv()

    def wait_rows(group):
        _, ups, downs = group

        @pl.when(row < last)
        def _():
            for item in ups:
                item.wait_recv()

        @pl.when(row > 0)
        def _():
            for item in downs:
                item.wait_recv()

    def wait_send(group):
        side, ups, downs = group
        side.wait_send()

        @pl.when(row > 0)
        def _():
            for item in ups:
                item.wait_send()

        @pl.when(row < last)
        def _():
            for item in downs:
                item.wait_send()

    def by_row(field):
        return jnp.swapaxes(field.astype(F32), 0, 1)

    mid = pl.ds(RIM, rows)
    own = pl.ds(0, width)
    low, high = pl.ds(0, half), pl.ds(half, half)
    loads[0].wait()
    z_one[mid, low, own] = by_row(inputs[0]).astype(BF16)
    loads[1].wait()
    z_one[mid, high, own] = by_row(hidden_init[...]).astype(BF16)
    for at, rim in ((0, pl.ds(0, RIM)), (last, pl.ds(rows + RIM, RIM))):

        @pl.when(row == at)
        def _():
            for buf in (z_one, z_two, d_one, d_two):
                buf[rim] = jnp.zeros((RIM,) + buf.shape[1:], BF16)

    pl.semaphore_wait(barrier, 1 + 2 * has_up.astype(jnp.int32) + 2 * has_down.astype(jnp.int32))
    first_rim = copies(z_one, 0, chans, 0)
    input_rim = copies(z_two, 0, half, 1)
    hidden_rim = copies(z_two, half, half, 2)
    two_rim = copies(d_two, 0, half, 3)
    one_rim = copies(d_one, 0, half, 4)
    start(first_rim)

    for item in loads[2:]:
        item.wait()
    z_two[mid, low, own] = by_row(inputs[1]).astype(BF16)
    cell_zero[...] = by_row(cell_init[...])
    hid_grad[...] = by_row(grad_hidden[...])
    cel_grad[...] = by_row(grad_cell[...])
    point_t[...] = jnp.transpose(point_kernel[...].astype(F32)).astype(BF16)
    bias_wide[...] = jnp.broadcast_to(jnp.transpose(gate_bias[...]), bias_wide.shape)
    tap_cols = jnp.transpose(depth_kernel[...])
    for tap in range(25):
        taps[tap] = jnp.broadcast_to(tap_cols[:, tap : tap + 1], taps.shape[1:])
    bias_part[...] = jnp.zeros_like(bias_part)

    lane = lax.broadcasted_iota(jnp.int32, (half, LANES), 1)
    least = col * (LANES - RIM)
    keep = jnp.logical_and(lane >= least, lane < least + RIM)

    def shift_mid(buf, first, into):
        shift_rows(buf, first, into, RIM, rows)

    def shift_ends(buf, first, into):
        shift_rows(buf, first, into, 0, RIM)
        shift_rows(buf, first, into, rows + RIM, RIM)

    def shift_rows(buf, first, into, begin, count):
        ch = pl.ds(first, half)

        @pl.loop(begin, begin + count, unroll=2)
        def _(at):
            mine = buf[at, ch, own].astype(F32)
            side = jnp.where(keep, buf[at, ch, beyond].astype(F32), 0.0)
            ring = jnp.concatenate([mine, side], axis=1)
            for tap in range(5):
                moved = pltpu.roll(ring, (RIM - tap) % ring.shape[1], 1) if tap != RIM else ring
                into[tap, at, ch, :] = moved[:, :width]

    inner = [(RIM, rows - 2 * RIM)]
    outer = [(0, RIM), (rows - RIM, RIM)]

    def tap_sum(source, group, weight_at, flip, begin, count):
        ch = pl.ds(pl.multiple_of(group * 8, 8), 8)
        wch = pl.ds(pl.multiple_of(weight_at + group * 8, 8), 8)
        total = None
        for col_tap in range(5):
            for row_tap in range(5):
                tap = row_tap * 5 + col_tap
                weight = taps[24 - tap if flip else tap, wch, :]
                term = weight[None] * source[col_tap, pl.ds(begin + row_tap, count), ch, :]
                total = term if total is None else total + term
        return total, ch

    def depth_of(source, groups, parts):
        @pl.loop(*groups)
        def _(group):
            for begin, count in parts:
                total, ch = tap_sum(source, group, 0, False, begin, count)
                for at in range(count):
                    depth_wide[ch, pl.ds((begin + at) * width, width)] = total[at]

    def spread_of(parts):
        @pl.loop(0, half // 8)
        def _(group):
            for begin, count in parts:
                total, ch = tap_sum(shift_back, group, half, True, begin, count)
                spread[pl.ds(begin, count), ch, :] = total

    def gates_at(at, cells):
        low_depth = depth_wide[:, cells].astype(BF16)
        gates = jnp.dot(point_t[...], low_depth, preferred_element_type=F32) + bias_wide[...]
        i = sigmoid(gates[:half])
        f = sigmoid(gates[half : 2 * half])
        o = sigmoid(gates[2 * half : 3 * half])
        u = jnp.tanh(gates[3 * half :])
        return low_depth, i, f, o, u

    def cells_of(at):
        return pl.ds(pl.multiple_of(at * width, width), width)

    def back_at(at, d_buf, which, i, f, o, u, th, prev, dh, dc):
        dc = dc + dh * o * (1.0 - th * th)
        dg = jnp.concatenate(
            [
                dc * u * i * (1.0 - i),
                dc * prev * f * (1.0 - f),
                dh * th * o * (1.0 - o),
                dc * i * (1.0 - u * u),
            ],
            axis=0,
        )
        bias_part[...] += dg
        dg_low = dg.astype(BF16)
        grads_low[which, :, cells_of(at)] = dg_low
        dd = jnp.dot(point_kernel[...], dg_low, preferred_element_type=F32).astype(BF16)
        d_buf[at + RIM, :, own] = dd[half:]
        depth_grad[at] = dd.astype(F32)
        return dc * f

    def kernel_grad(source, begin):
        @pl.loop(0, chans // 8)
        def _(group):
            ch = pl.ds(pl.multiple_of(group * 8, 8), 8)
            grad = depth_grad[:, ch, :]
            for col_tap in range(5):
                for row_tap in range(5):
                    tap = row_tap * 5 + col_tap
                    both = jnp.sum(grad * source[col_tap, pl.ds(row_tap, rows), ch, :], axis=0)
                    part = both[:, :LANES]
                    for tile in range(1, width // LANES):
                        part = part + both[:, tile * LANES : (tile + 1) * LANES]
                    if begin:
                        tap_part[tap, ch, :] = part
                    else:
                        tap_part[tap, ch, :] += part

    def point_grad(which):
        return lax.dot_general(
            depth_low[which], grads_low[which], (((1,), (1,)), ((), ())), preferred_element_type=F32
        )

    every, first, second = (0, chans // 8), (0, half // 8), (half // 8, chans // 8)
    wait_side(first_rim)
    shift_mid(z_one, 0, shift_one)
    shift_mid(z_one, half, shift_one)
    depth_of(shift_one, every, inner)
    wait_rows(first_rim)
    start(input_rim)
    tell_far(0)
    shift_ends(z_one, 0, shift_one)
    shift_ends(z_one, half, shift_one)
    depth_of(shift_one, every, outer)

    @pl.loop(0, rows, unroll=True)
    def _(at):
        cells = cells_of(at)
        low_depth, i, f, o, u = gates_at(at, cells)
        depth_low[0, :, cells] = low_depth
        c = f * cell_zero[at] + i * u
        th = jnp.tanh(c)
        z_two[at + RIM, high, own] = (o * th).astype(BF16)
        gates_one[at] = jnp.concatenate([i, f, o, u], axis=0)
        cell_one[at] = c
        tanh_one[at] = th

    start(hidden_rim)

    wait_side(input_rim)
    wait_rows(input_rim)
    shift_mid(z_two, 0, shift_two)
    shift_ends(z_two, 0, shift_two)
    depth_of(shift_two, first, inner + outer)
    wait_side(hidden_rim)
    shift_mid(z_two, half, shift_two)
    depth_of(shift_two, second, inner)
    wait_rows(hidden_rim)
    hear_far(0)
    for level in range(1, len(distances)):
        if level > 1:
            hear_far(level - 1)
        tell_far(level)
    shift_ends(z_two, half, shift_two)
    depth_of(shift_two, second, outer)

    @pl.loop(0, rows, unroll=True)
    def _(at):
        cells = cells_of(at)
        low_depth, i, f, o, u = gates_at(at, cells)
        depth_low[1, :, cells] = low_depth
        prev = cell_one[at]
        th = jnp.tanh(f * prev + i * u)
        cel_grad[at] = back_at(at, d_two, 1, i, f, o, u, th, prev, hid_grad[at], cel_grad[at])

    start(two_rim)
    kernel_grad(shift_two, True)
    wait_side(two_rim)
    shift_mid(d_two, 0, shift_back)
    spread_of(inner)
    point_part[...] = point_grad(1)
    wait_rows(two_rim)
    if len(distances) > 1:
        hear_far(len(distances) - 1)
    shift_ends(d_two, 0, shift_back)
    spread_of(outer)

    @pl.loop(0, rows, unroll=True)
    def _(at):
        held = gates_one[at]
        i, f, o, u = (held[q * half : (q + 1) * half] for q in range(4))
        cel_grad[at] = back_at(
            at, d_one, 0, i, f, o, u, tanh_one[at], cell_zero[at], spread[at], cel_grad[at]
        )

    start(one_rim)
    kernel_grad(shift_one, False)
    point = (point_part[...] + point_grad(0)) * scale

    wide_lane = lax.broadcasted_iota(jnp.int32, (chans, LANES), 1)
    extra = jnp.zeros((chans, LANES), F32)
    for tap in range(25):
        sums = jnp.sum(tap_part[tap], axis=1, keepdims=True)
        extra = jnp.where(wide_lane == tap, sums, extra)
    bias_sum = jnp.sum(bias_part[...], axis=1, keepdims=True)
    extra = jnp.where(wide_lane == 25, bias_sum[:chans], extra)
    extra = jnp.where(wide_lane == 26, bias_sum[chans:], extra)
    pay[pl.ds(0, owners // 2)] = point.reshape(owners // 2, chunk, LANES)
    pay[pl.ds(owners // 2, owners // 2)] = (extra * scale).reshape(owners // 2, chunk, LANES)

    def scatter(k):
        owner = lax.rem(me + n - k, n)
        slot = jnp.minimum(owner, owners - 1)
        return owner, pltpu.make_async_remote_copy(
            src_ref=pay.at[slot],
            dst_ref=arrived.at[k - 1],
            send_sem=sum_send.at[k - 1],
            recv_sem=sum_recv.at[k - 1],
            device_id=place(owner),
            device_id_type=MESH,
        )

    def gather(k):
        return pltpu.make_async_remote_copy(
            src_ref=gathered.at[jnp.minimum(me, owners - 1)],
            dst_ref=gathered.at[jnp.minimum(me, owners - 1)],
            send_sem=all_send.at[k - 1],
            recv_sem=all_recv.at[k - 1],
            device_id=place(lax.rem(me + k, n)),
            device_id_type=MESH,
        )

    def owned(index, body):
        if owners == n:
            body()
        else:
            pl.when(index < owners)(body)

    @pl.loop(1, n)
    def _(k):
        owner, item = scatter(k)
        owned(owner, item.start)

    out_cell[...] = jnp.swapaxes(cel_grad[...], 0, 1).astype(BF16)
    wait_side(one_rim)
    shift_mid(d_one, 0, shift_back)
    spread_of(inner)
    wait_rows(one_rim)
    shift_ends(d_one, 0, shift_back)
    spread_of(outer)
    out_hidden[...] = jnp.swapaxes(spread[...], 0, 1).astype(BF16)

    def reduce_own():
        @pl.loop(1, n)
        def _(k):
            scatter(k)[1].wait_recv()

        total = pay[jnp.minimum(me, owners - 1)] + jnp.sum(arrived[...], axis=0)
        gathered[jnp.minimum(me, owners - 1)] = total

        @pl.loop(1, n)
        def _(k):
            gather(k).start()

    owned(me, reduce_own)

    @pl.loop(1, n)
    def _(k):
        owned(lax.rem(me + n - k, n), lambda: gather(k).wait_recv())

    out_point[...] = gathered[pl.ds(0, owners // 2)].reshape(chans, LANES)
    rest = gathered[pl.ds(owners // 2, owners // 2)].reshape(chans, LANES)
    turned = jnp.transpose(rest)
    out_depth[...] = turned[:25]
    out_bias[...] = jnp.concatenate([turned[25:26], turned[26:27]], axis=1)

    for group in (first_rim, input_rim, hidden_rim, two_rim, one_rim):
        wait_send(group)

    @pl.loop(1, n)
    def _(k):
        owner, item = scatter(k)
        owned(owner, item.wait_send)

    def drain():
        @pl.loop(1, n)
        def _(k):
            gather(k).wait_send()

    owned(me, drain)


def hand_over(*refs):
    sems = refs[10]
    items = [pltpu.make_async_copy(refs[at], refs[5 + at], sems.at[at]) for at in range(5)]
    for item in items:
        item.start()
    for item in items:
        item.wait()


def arrived_shape(n):
    owners = min(n, 16)
    return owners, LANES // owners


def local(
    inputs, hidden_init, cell_init, grad_hidden, grad_cell, depth_kernel, point_kernel, gate_bias
):
    half, rows, width = hidden_init.shape
    chans = 2 * half
    n_rows, n_cols = lax.axis_size("rows"), lax.axis_size("cols")
    n = n_rows * n_cols
    owners, chunk = arrived_shape(n)
    scale = 1.0 / math.sqrt(rows * width * n)
    tall, wide = rows + 2 * RIM, width + LANES
    gates = 4 * half
    vm = pltpu.VMEM
    dma = pltpu.SemaphoreType.DMA
    outs = pl.pallas_call(
        functools.partial(kernel, (n_rows, n_cols, rows, width, chans, scale)),
        out_shape=[
            jax.ShapeDtypeStruct((half, rows, width), BF16),
            jax.ShapeDtypeStruct((half, rows, width), BF16),
            jax.ShapeDtypeStruct((chans, gates), F32),
            jax.ShapeDtypeStruct((25, chans), F32),
            jax.ShapeDtypeStruct((1, gates), F32),
        ],
        in_specs=[pl.BlockSpec(memory_space=pltpu.HBM)] * 8,
        out_specs=[pl.BlockSpec(memory_space=pltpu.VMEM)] * 5,
        scratch_shapes=[
            vm(inputs.shape, BF16),
            vm((half, rows, width), BF16),
            vm((half, rows, width), BF16),
            vm((half, rows, width), BF16),
            vm((half, rows, width), BF16),
            vm((25, chans), F32),
            vm((chans, gates), BF16),
            vm((1, gates), F32),
            vm((tall, chans, wide), BF16),
            vm((tall, chans, wide), BF16),
            vm((tall, half, wide), BF16),
            vm((tall, half, wide), BF16),
            vm((5, tall, chans, width), F32),
            vm((5, tall, chans, width), F32),
            vm((5, tall, half, width), F32),
            vm((25, chans, width), F32),
            vm((chans, rows * width), F32),
            vm((2, chans, rows * width), BF16),
            vm((2, gates, rows * width), BF16),
            vm((gates, chans), BF16),
            vm((gates, width), F32),
            vm((rows, gates, width), F32),
            vm((rows, half, width), F32),
            vm((rows, half, width), F32),
            vm((rows, half, width), F32),
            vm((rows, half, width), F32),
            vm((rows, half, width), F32),
            vm((rows, half, width), F32),
            vm((rows, chans, width), F32),
            vm((25, chans, LANES), F32),
            vm((gates, width), F32),
            vm((chans, gates), F32),
            vm((owners, chunk, LANES), F32),
            vm((owners, chunk, LANES), F32),
            vm((n - 1, chunk, LANES), F32),
            dma((5, 5)),
            dma((5, 5)),
            dma((n - 1,)),
            dma((n - 1,)),
            dma((n - 1,)),
            dma((n - 1,)),
            dma((9,)),
            pltpu.SemaphoreType.REGULAR((max(1, (n_rows - 1).bit_length() - 1),)),
        ],
        compiler_params=pltpu.CompilerParams(
            collective_id=0, has_side_effects=True, vmem_limit_bytes=64 * 1024 * 1024 - 65536
        ),
        name="surrogate",
    )(
        inputs, hidden_init, cell_init, grad_hidden, grad_cell, depth_kernel.T, point_kernel,
        gate_bias.reshape(1, -1),
    )
    outs = pl.pallas_call(
        hand_over,
        out_shape=[jax.ShapeDtypeStruct(out.shape, out.dtype) for out in outs],
        in_specs=[pl.BlockSpec(memory_space=pltpu.VMEM)] * 5,
        out_specs=[pl.BlockSpec(memory_space=pltpu.HBM)] * 5,
        scratch_shapes=[dma((5,))],
        name="hand_over",
    )(*outs)
    return (*outs[:3], outs[3].T, outs[4].reshape(-1))


def solution(mesh):
    placed = (
        P("groups", None, "rows", "cols"),
        P("groups", "rows", "cols"),
        P("groups", "rows", "cols"),
        P("groups", "rows", "cols"),
        P("groups", "rows", "cols"),
        P(),
        P(),
        P(),
    )
    return jax.shard_map(
        local,
        mesh=mesh,
        in_specs=placed,
        out_specs=(
            P("groups", "rows", "cols"),
            P("groups", "rows", "cols"),
            P("groups", None),
            P("groups", None),
            P("groups"),
        ),
        check_vma=False,
    )
```

```python
import functools
import math

import jax
import jax.numpy as jnp
from jax import lax
from jax.experimental import pallas as pl
from jax.experimental.pallas import tpu as pltpu
from jax.sharding import PartitionSpec as P

F32 = jnp.float32
BF16 = jnp.bfloat16
MESH = pl.DeviceIdType.MESH
LANES = 128
RIM = 2


def sigmoid(x):
    return 0.5 * jnp.tanh(0.5 * x) + 0.5


def kernel(
    dims,
    inputs_hbm, hidden_hbm, cell_hbm, grad_hidden_hbm, grad_cell_hbm, depth_hbm, point_hbm, bias_hbm,
    out_hidden, out_cell, out_point, out_depth, out_bias,
    inputs, hidden_init, cell_init, grad_hidden, grad_cell, depth_kernel, point_kernel, gate_bias,
    z_one, z_two, d_one, d_two, corner_out, corner_in,
    shift_one, shift_two, shift_back,
    taps, depth_wide, depth_low, grads_low, point_t, bias_wide,
    gates_one, cell_zero, cell_one, tanh_one, hid_grad, cel_grad, spread,
    depth_grad, tap_part, bias_part, point_part,
    pay, gathered, arrived,
    rim_send, rim_recv, sum_send, sum_recv, all_send, all_recv, load_sem, known,
):
    n_rows, n_cols, rows, width, chans, scale = dims
    half = chans // 2
    n = n_rows * n_cols
    owners, chunk = arrived_shape(n)
    row = lax.axis_index("rows")
    col = lax.axis_index("cols")
    me = row * n_cols + col
    last = n_rows - 1
    edge = pl.ds(pl.multiple_of((1 - col) * (width - LANES), LANES), LANES)
    beyond = pl.ds(width, LANES)

    def place(index):
        return {"rows": index // n_cols, "cols": lax.rem(index, n_cols)}

    barrier = pltpu.get_barrier_semaphore()

    has_up, has_down = row > 0, row < last

    def tell(sem, to_row, to_col):
        pl.semaphore_signal(
            sem, inc=1, device_id={"rows": to_row, "cols": to_col}, device_id_type=MESH
        )

    tell(barrier, row, 1 - col)

    @pl.when(has_up)
    def _():
        tell(barrier, row - 1, col)
        tell(barrier, row - 1, 1 - col)

    @pl.when(has_down)
    def _():
        tell(barrier, row + 1, col)
        tell(barrier, row + 1, 1 - col)

    loads = [
        pltpu.make_async_copy(src, dst, load_sem.at[at])
        for at, (src, dst) in enumerate(
            [
                (inputs_hbm.at[0], inputs.at[0]),
                (hidden_hbm, hidden_init),
                (inputs_hbm.at[1], inputs.at[1]),
                (cell_hbm, cell_init),
                (grad_hidden_hbm, grad_hidden),
                (grad_cell_hbm, grad_cell),
                (depth_hbm, depth_kernel),
                (point_hbm, point_kernel),
                (bias_hbm, gate_bias),
            ]
        )
    ]
    for item in loads:
        item.start()

    distances = [d for d in (2**p for p in range(1, 16)) if d < n_rows]

    def tell_far(level):
        d = distances[level]
        for ahead, to_row in ((row >= d, row - d), (row + d <= last, row + d)):

            @pl.when(ahead)
            def _():
                tell(known.at[level], jnp.clip(to_row, 0, last), col)

    def hear_far(level):
        d = distances[level]
        count = (row >= d).astype(jnp.int32) + (row + d <= last).astype(jnp.int32)
        pl.semaphore_wait(known.at[level], count)

    def copies(buf, first, count, which):
        ch = pl.ds(first, count)
        own = pl.ds(0, width)
        up_src, up_dst = pl.ds(RIM, RIM), pl.ds(rows + RIM, RIM)
        down_src, down_dst = pl.ds(rows, RIM), pl.ds(0, RIM)
        mid = pl.ds(RIM, rows)

        def one(at, src_rows, dst_rows, src_cols, dst_cols, to_row, to_col):
            return pltpu.make_async_remote_copy(
                src_ref=buf.at[src_rows, ch, src_cols],
                dst_ref=buf.at[dst_rows, ch, dst_cols],
                send_sem=rim_send.at[which, at],
                recv_sem=rim_recv.at[which, at],
                device_id={"rows": to_row, "cols": to_col},
                device_id_type=MESH,
            )

        def corner(at, way, to_row):
            held = pl.ds(0, count // 2)
            return pltpu.make_async_remote_copy(
                src_ref=corner_out.at[which, way, held],
                dst_ref=corner_in.at[which, way, held],
                send_sem=rim_send.at[which, at],
                recv_sem=rim_recv.at[which, at],
                device_id={"rows": to_row, "cols": 1 - col},
                device_id_type=MESH,
            )

        above, below = jnp.maximum(row - 1, 0), jnp.minimum(row + 1, last)
        side = one(0, mid, mid, edge, beyond, row, 1 - col)
        ups = [
            one(1, up_src, up_dst, own, own, above, col),
            corner(2, 0, above),
        ]
        downs = [
            one(3, down_src, down_dst, own, own, below, col),
            corner(4, 1, below),
        ]
        return side, ups, downs, (buf, first, count, which)

    lanes = lax.broadcasted_iota(jnp.int32, (chans // 2, LANES), 1)
    strip = LANES // 4

    def pack(buf, first, count, which):
        part = count // 2
        for way, begin in ((0, RIM), (1, rows)):
            tile = None
            for q in range(4):
                piece = buf[begin + q // 2, pl.ds(first + q % 2 * part, part), edge].astype(F32)
                if q == 0:
                    tile = piece
                else:
                    place_in = lanes[:part] - (1 - col) * (LANES - RIM) - q * strip + 2 * LANES
                    taken = jnp.bitwise_and(place_in, LANES - 1) < RIM
                    tile = jnp.where(taken, pltpu.roll(piece, q * strip, 1), tile)
            corner_out[which, way, pl.ds(0, part), :] = tile.astype(BF16)

    def unpack(way, begin, buf, first, count, which):
        part = count // 2
        tile = corner_in[which, way, pl.ds(0, part), :].astype(F32)
        for q in range(4):
            piece = pltpu.roll(tile, LANES - q * strip, 1) if q else tile
            buf[begin + q // 2, pl.ds(first + q % 2 * part, part), beyond] = piece.astype(BF16)

    def start(group):
        side, ups, downs, what = group
        side.start()
        for item, there in ((ups[0], row > 0), (downs[0], row < last)):
            pl.when(there)(item.start)
        pack(*what)

        @pl.when(row > 0)
        def _():
            ups[1].start()

        @pl.when(row < last)
        def _():
            downs[1].start()

    def wait_side(group):
        group[0].wait_recv()

    def wait_rows(group):
        _, ups, downs, what = group

        @pl.when(row < last)
        def _():
            for item in ups:
                item.wait_recv()
            unpack(0, rows + RIM, *what)

        @pl.when(row > 0)
        def _():
            for item in downs:
                item.wait_recv()
            unpack(1, 0, *what)

    def wait_send(group):
        side, ups, downs, _ = group
        side.wait_send()

        @pl.when(row > 0)
        def _():
            for item in ups:
                item.wait_send()

        @pl.when(row < last)
        def _():
            for item in downs:
                item.wait_send()

    def by_row(field):
        return jnp.swapaxes(field.astype(F32), 0, 1)

    mid = pl.ds(RIM, rows)
    own = pl.ds(0, width)
    low, high = pl.ds(0, half), pl.ds(half, half)
    loads[0].wait()
    z_one[mid, low, own] = by_row(inputs[0]).astype(BF16)
    loads[1].wait()
    z_one[mid, high, own] = by_row(hidden_init[...]).astype(BF16)
    for at, rim in ((0, pl.ds(0, RIM)), (last, pl.ds(rows + RIM, RIM))):

        @pl.when(row == at)
        def _():
            for buf in (z_one, z_two, d_one, d_two):
                buf[rim] = jnp.zeros((RIM,) + buf.shape[1:], BF16)

    pl.semaphore_wait(barrier, 1 + 2 * has_up.astype(jnp.int32) + 2 * has_down.astype(jnp.int32))
    first_rim = copies(z_one, 0, chans, 0)
    input_rim = copies(z_two, 0, half, 1)
    hidden_rim = copies(z_two, half, half, 2)
    two_rim = copies(d_two, 0, half, 3)
    one_rim = copies(d_one, 0, half, 4)
    start(first_rim)

    for item in loads[2:]:
        item.wait()
    z_two[mid, low, own] = by_row(inputs[1]).astype(BF16)
    cell_zero[...] = by_row(cell_init[...])
    hid_grad[...] = by_row(grad_hidden[...])
    cel_grad[...] = by_row(grad_cell[...])
    point_t[...] = jnp.transpose(point_kernel[...].astype(F32)).astype(BF16)
    bias_wide[...] = jnp.broadcast_to(jnp.transpose(gate_bias[...]), bias_wide.shape)
    tap_cols = jnp.transpose(depth_kernel[...])
    for tap in range(25):
        taps[tap] = jnp.broadcast_to(tap_cols[:, tap : tap + 1], taps.shape[1:])
    bias_part[...] = jnp.zeros_like(bias_part)

    lane = lax.broadcasted_iota(jnp.int32, (half, LANES), 1)
    least = col * (LANES - RIM)
    keep = jnp.logical_and(lane >= least, lane < least + RIM)

    def shift_mid(buf, first, into):
        shift_rows(buf, first, into, RIM, rows)

    def shift_ends(buf, first, into):
        shift_rows(buf, first, into, 0, RIM)
        shift_rows(buf, first, into, rows + RIM, RIM)

    def shift_rows(buf, first, into, begin, count):
        ch = pl.ds(first, half)

        @pl.loop(begin, begin + count, unroll=2)
        def _(at):
            mine = buf[at, ch, own].astype(F32)
            side = jnp.where(keep, buf[at, ch, beyond].astype(F32), 0.0)
            ring = jnp.concatenate([mine, side], axis=1)
            for tap in range(5):
                moved = pltpu.roll(ring, (RIM - tap) % ring.shape[1], 1) if tap != RIM else ring
                into[tap, at, ch, :] = moved[:, :width]

    inner = [(RIM, rows - 2 * RIM)]
    outer = [(0, RIM), (rows - RIM, RIM)]

    def tap_sum(source, group, weight_at, flip, begin, count):
        ch = pl.ds(pl.multiple_of(group * 8, 8), 8)
        wch = pl.ds(pl.multiple_of(weight_at + group * 8, 8), 8)
        total = None
        for col_tap in range(5):
            for row_tap in range(5):
                tap = row_tap * 5 + col_tap
                weight = taps[24 - tap if flip else tap, wch, :]
                term = weight[None] * source[col_tap, pl.ds(begin + row_tap, count), ch, :]
                total = term if total is None else total + term
        return total, ch

    def depth_of(source, groups, parts):
        @pl.loop(*groups)
        def _(group):
            for begin, count in parts:
                total, ch = tap_sum(source, group, 0, False, begin, count)
                for at in range(count):
                    depth_wide[ch, pl.ds((begin + at) * width, width)] = total[at]

    def spread_of(parts):
        @pl.loop(0, half // 8)
        def _(group):
            for begin, count in parts:
                total, ch = tap_sum(shift_back, group, half, True, begin, count)
                spread[pl.ds(begin, count), ch, :] = total

    def gates_at(at, cells):
        low_depth = depth_wide[:, cells].astype(BF16)
        gates = jnp.dot(point_t[...], low_depth, preferred_element_type=F32) + bias_wide[...]
        i = sigmoid(gates[:half])
        f = sigmoid(gates[half : 2 * half])
        o = sigmoid(gates[2 * half : 3 * half])
        u = jnp.tanh(gates[3 * half :])
        return low_depth, i, f, o, u

    def cells_of(at):
        return pl.ds(pl.multiple_of(at * width, width), width)

    def back_at(at, d_buf, which, i, f, o, u, th, prev, dh, dc):
        dc = dc + dh * o * (1.0 - th * th)
        dg = jnp.concatenate(
            [
                dc * u * i * (1.0 - i),
                dc * prev * f * (1.0 - f),
                dh * th * o * (1.0 - o),
                dc * i * (1.0 - u * u),
            ],
            axis=0,
        )
        bias_part[...] += dg
        dg_low = dg.astype(BF16)
        grads_low[which, :, cells_of(at)] = dg_low
        dd = jnp.dot(point_kernel[...], dg_low, preferred_element_type=F32).astype(BF16)
        d_buf[at + RIM, :, own] = dd[half:]
        depth_grad[at] = dd.astype(F32)
        return dc * f

    def kernel_grad(source, begin):
        @pl.loop(0, chans // 8)
        def _(group):
            ch = pl.ds(pl.multiple_of(group * 8, 8), 8)
            grad = depth_grad[:, ch, :]
            for col_tap in range(5):
                for row_tap in range(5):
                    tap = row_tap * 5 + col_tap
                    both = jnp.sum(grad * source[col_tap, pl.ds(row_tap, rows), ch, :], axis=0)
                    part = both[:, :LANES]
                    for tile in range(1, width // LANES):
                        part = part + both[:, tile * LANES : (tile + 1) * LANES]
                    if begin:
                        tap_part[tap, ch, :] = part
                    else:
                        tap_part[tap, ch, :] += part

    def point_grad(which):
        return lax.dot_general(
            depth_low[which], grads_low[which], (((1,), (1,)), ((), ())), preferred_element_type=F32
        )

    every, first, second = (0, chans // 8), (0, half // 8), (half // 8, chans // 8)
    wait_side(first_rim)
    shift_mid(z_one, 0, shift_one)
    shift_mid(z_one, half, shift_one)
    depth_of(shift_one, every, inner)
    wait_rows(first_rim)
    start(input_rim)
    tell_far(0)
    shift_ends(z_one, 0, shift_one)
    shift_ends(z_one, half, shift_one)
    depth_of(shift_one, every, outer)

    @pl.loop(0, rows, unroll=True)
    def _(at):
        cells = cells_of(at)
        low_depth, i, f, o, u = gates_at(at, cells)
        depth_low[0, :, cells] = low_depth
        c = f * cell_zero[at] + i * u
        th = jnp.tanh(c)
        z_two[at + RIM, high, own] = (o * th).astype(BF16)
        gates_one[at] = jnp.concatenate([i, f, o, u], axis=0)
        cell_one[at] = c
        tanh_one[at] = th

    start(hidden_rim)

    wait_side(input_rim)
    wait_rows(input_rim)
    shift_mid(z_two, 0, shift_two)
    shift_ends(z_two, 0, shift_two)
    depth_of(shift_two, first, inner + outer)
    wait_side(hidden_rim)
    shift_mid(z_two, half, shift_two)
    depth_of(shift_two, second, inner)
    wait_rows(hidden_rim)
    hear_far(0)
    for level in range(1, len(distances)):
        if level > 1:
            hear_far(level - 1)
        tell_far(level)
    shift_ends(z_two, half, shift_two)
    depth_of(shift_two, second, outer)

    @pl.loop(0, rows, unroll=True)
    def _(at):
        cells = cells_of(at)
        low_depth, i, f, o, u = gates_at(at, cells)
        depth_low[1, :, cells] = low_depth
        prev = cell_one[at]
        th = jnp.tanh(f * prev + i * u)
        cel_grad[at] = back_at(at, d_two, 1, i, f, o, u, th, prev, hid_grad[at], cel_grad[at])

    start(two_rim)
    kernel_grad(shift_two, True)
    wait_side(two_rim)
    shift_mid(d_two, 0, shift_back)
    spread_of(inner)
    point_part[...] = point_grad(1)
    wait_rows(two_rim)
    if len(distances) > 1:
        hear_far(len(distances) - 1)
    shift_ends(d_two, 0, shift_back)
    spread_of(outer)

    @pl.loop(0, rows, unroll=True)
    def _(at):
        held = gates_one[at]
        i, f, o, u = (held[q * half : (q + 1) * half] for q in range(4))
        cel_grad[at] = back_at(
            at, d_one, 0, i, f, o, u, tanh_one[at], cell_zero[at], spread[at], cel_grad[at]
        )

    start(one_rim)
    kernel_grad(shift_one, False)
    point = (point_part[...] + point_grad(0)) * scale

    wide_lane = lax.broadcasted_iota(jnp.int32, (chans, LANES), 1)
    extra = jnp.zeros((chans, LANES), F32)
    for tap in range(25):
        sums = jnp.sum(tap_part[tap], axis=1, keepdims=True)
        extra = jnp.where(wide_lane == tap, sums, extra)
    bias_sum = jnp.sum(bias_part[...], axis=1, keepdims=True)
    extra = jnp.where(wide_lane == 25, bias_sum[:chans], extra)
    extra = jnp.where(wide_lane == 26, bias_sum[chans:], extra)
    pay[pl.ds(0, owners // 2)] = point.reshape(owners // 2, chunk, LANES)
    pay[pl.ds(owners // 2, owners // 2)] = (extra * scale).reshape(owners // 2, chunk, LANES)

    def scatter(k):
        owner = lax.rem(me + n - k, n)
        slot = jnp.minimum(owner, owners - 1)
        return owner, pltpu.make_async_remote_copy(
            src_ref=pay.at[slot],
            dst_ref=arrived.at[k - 1],
            send_sem=sum_send.at[k - 1],
            recv_sem=sum_recv.at[k - 1],
            device_id=place(owner),
            device_id_type=MESH,
        )

    def gather(k):
        return pltpu.make_async_remote_copy(
            src_ref=gathered.at[jnp.minimum(me, owners - 1)],
            dst_ref=gathered.at[jnp.minimum(me, owners - 1)],
            send_sem=all_send.at[k - 1],
            recv_sem=all_recv.at[k - 1],
            device_id=place(lax.rem(me + k, n)),
            device_id_type=MESH,
        )

    def owned(index, body):
        if owners == n:
            body()
        else:
            pl.when(index < owners)(body)

    @pl.loop(1, n)
    def _(k):
        owner, item = scatter(k)
        owned(owner, item.start)

    out_cell[...] = jnp.swapaxes(cel_grad[...], 0, 1).astype(BF16)
    wait_side(one_rim)
    shift_mid(d_one, 0, shift_back)
    spread_of(inner)

    def reduce_own():
        @pl.loop(1, n)
        def _(k):
            scatter(k)[1].wait_recv()

        total = pay[jnp.minimum(me, owners - 1)] + jnp.sum(arrived[...], axis=0)
        gathered[jnp.minimum(me, owners - 1)] = total

        @pl.loop(1, n)
        def _(k):
            gather(k).start()

    owned(me, reduce_own)
    wait_rows(one_rim)
    shift_ends(d_one, 0, shift_back)
    spread_of(outer)
    out_hidden[...] = jnp.swapaxes(spread[...], 0, 1).astype(BF16)

    @pl.loop(1, n)
    def _(k):
        owned(lax.rem(me + n - k, n), lambda: gather(k).wait_recv())

    out_point[...] = gathered[pl.ds(0, owners // 2)].reshape(chans, LANES)
    rest = gathered[pl.ds(owners // 2, owners // 2)].reshape(chans, LANES)
    turned = jnp.transpose(rest)
    out_depth[...] = turned[:25]
    out_bias[...] = jnp.concatenate([turned[25:26], turned[26:27]], axis=1)

    for group in (first_rim, input_rim, hidden_rim, two_rim, one_rim):
        wait_send(group)

    @pl.loop(1, n)
    def _(k):
        owner, item = scatter(k)
        owned(owner, item.wait_send)

    def drain():
        @pl.loop(1, n)
        def _(k):
            gather(k).wait_send()

    owned(me, drain)


def hand_over(*refs):
    sems = refs[10]
    items = [pltpu.make_async_copy(refs[at], refs[5 + at], sems.at[at]) for at in range(5)]
    for item in items:
        item.start()
    for item in items:
        item.wait()


def arrived_shape(n):
    owners = min(n, 16)
    return owners, LANES // owners


def local(
    inputs, hidden_init, cell_init, grad_hidden, grad_cell, depth_kernel, point_kernel, gate_bias
):
    half, rows, width = hidden_init.shape
    chans = 2 * half
    n_rows, n_cols = lax.axis_size("rows"), lax.axis_size("cols")
    n = n_rows * n_cols
    owners, chunk = arrived_shape(n)
    scale = 1.0 / math.sqrt(rows * width * n)
    tall, wide = rows + 2 * RIM, width + LANES
    gates = 4 * half
    vm = pltpu.VMEM
    dma = pltpu.SemaphoreType.DMA
    outs = pl.pallas_call(
        functools.partial(kernel, (n_rows, n_cols, rows, width, chans, scale)),
        out_shape=[
            jax.ShapeDtypeStruct((half, rows, width), BF16),
            jax.ShapeDtypeStruct((half, rows, width), BF16),
            jax.ShapeDtypeStruct((chans, gates), F32),
            jax.ShapeDtypeStruct((25, chans), F32),
            jax.ShapeDtypeStruct((1, gates), F32),
        ],
        in_specs=[pl.BlockSpec(memory_space=pltpu.HBM)] * 8,
        out_specs=[pl.BlockSpec(memory_space=pltpu.VMEM)] * 5,
        scratch_shapes=[
            vm(inputs.shape, BF16),
            vm((half, rows, width), BF16),
            vm((half, rows, width), BF16),
            vm((half, rows, width), BF16),
            vm((half, rows, width), BF16),
            vm((25, chans), F32),
            vm((chans, gates), BF16),
            vm((1, gates), F32),
            vm((tall, chans, wide), BF16),
            vm((tall, chans, wide), BF16),
            vm((tall, half, wide), BF16),
            vm((tall, half, wide), BF16),
            vm((5, 2, chans // 2, LANES), BF16),
            vm((5, 2, chans // 2, LANES), BF16),
            vm((5, tall, chans, width), F32),
            vm((5, tall, chans, width), F32),
            vm((5, tall, half, width), F32),
            vm((25, chans, width), F32),
            vm((chans, rows * width), F32),
            vm((2, chans, rows * width), BF16),
            vm((2, gates, rows * width), BF16),
            vm((gates, chans), BF16),
            vm((gates, width), F32),
            vm((rows, gates, width), F32),
            vm((rows, half, width), F32),
            vm((rows, half, width), F32),
            vm((rows, half, width), F32),
            vm((rows, half, width), F32),
            vm((rows, half, width), F32),
            vm((rows, half, width), F32),
            vm((rows, chans, width), F32),
            vm((25, chans, LANES), F32),
            vm((gates, width), F32),
            vm((chans, gates), F32),
            vm((owners, chunk, LANES), F32),
            vm((owners, chunk, LANES), F32),
            vm((n - 1, chunk, LANES), F32),
            dma((5, 5)),
            dma((5, 5)),
            dma((n - 1,)),
            dma((n - 1,)),
            dma((n - 1,)),
            dma((n - 1,)),
            dma((9,)),
            pltpu.SemaphoreType.REGULAR((max(1, (n_rows - 1).bit_length() - 1),)),
        ],
        compiler_params=pltpu.CompilerParams(
            collective_id=0, has_side_effects=True, vmem_limit_bytes=64 * 1024 * 1024 - 65536
        ),
        name="surrogate",
    )(
        inputs, hidden_init, cell_init, grad_hidden, grad_cell, depth_kernel.T, point_kernel,
        gate_bias.reshape(1, -1),
    )
    outs = pl.pallas_call(
        hand_over,
        out_shape=[jax.ShapeDtypeStruct(out.shape, out.dtype) for out in outs],
        in_specs=[pl.BlockSpec(memory_space=pltpu.VMEM)] * 5,
        out_specs=[pl.BlockSpec(memory_space=pltpu.HBM)] * 5,
        scratch_shapes=[dma((5,))],
        name="hand_over",
    )(*outs)
    return (*outs[:3], outs[3].T, outs[4].reshape(-1))


def solution(mesh):
    placed = (
        P("groups", None, "rows", "cols"),
        P("groups", "rows", "cols"),
        P("groups", "rows", "cols"),
        P("groups", "rows", "cols"),
        P("groups", "rows", "cols"),
        P(),
        P(),
        P(),
    )
    return jax.shard_map(
        local,
        mesh=mesh,
        in_specs=placed,
        out_specs=(
            P("groups", "rows", "cols"),
            P("groups", "rows", "cols"),
            P("groups", None),
            P("groups", None),
            P("groups"),
        ),
        check_vma=False,
    )
```
